32 devices in a mesh: row: 8 (over z, x), col: 4 (over y, core).
Axes of the slice: x: 2, y: 2, z: 4, core: 2. Of those that a mesh axis runs over, the one named last changes fastest.
Arguments:
- slab: float32 [4096, 4096], P('row', 'col'), may hold values from -32 to 32, as said below
Outputs:
- factored: float32 [4096, 4096], P('row', 'col')
The draws below stay inside these ranges and needn't reach their ends.
Inputs may be any that keep to these rules, and one draw needn't show every extreme that they name: The slab holds the first 4096 columns of a symmetric positive definite matrix of order 4096, column blocks of 256 in the stored order of the first step.
All inputs are finite; a program needn't handle non-finite values.
Results may differ from the reference program's by a relative error of at most 0.00029.
Values sent between devices are 32-bit elements; how exact they have to be, the bound alone decides.
No kernel may reach another device: no remote copies, remote signals or barrier semaphores. Data moves between devices by JAX's collectives and lax.ppermute only.
A program may use at most 128 MiB of HBM per device.

```python
import jax
import jax.numpy as jnp
from jax import lax

SLAB_COLS = 4096
EMBED = 768
BLOCK = 256
PANELS = 2
ROWS_DEV = 512
N_ROW = 8
N_COL = 4


RIDGE_TERM = 0.5


def draw_slab(key, part):
    rows_all = ROWS_DEV * N_ROW
    samples = jax.random.normal(key, (rows_all, EMBED), jnp.float32)
    kernel = jnp.dot(samples, samples[:SLAB_COLS].T, precision=lax.Precision.HIGHEST, preferred_element_type=jnp.float32) / EMBED
    kernel = kernel + RIDGE_TERM * jnp.eye(rows_all, SLAB_COLS, dtype=jnp.float32)
    return kernel.reshape(rows_all, SLAB_COLS // (BLOCK * N_COL), N_COL, BLOCK).transpose(0, 2, 1, 3).reshape(rows_all, SLAB_COLS)


def setup_inputs(seed: int = 0) -> dict:
    keys = jax.random.split(jax.random.key(seed), 2)
    slab = draw_slab(jax.random.fold_in(keys[1], 71), 0)
    return dict(slab=slab)


PRECISE = lax.Precision.HIGHEST

def to_logical(stored):
    count = stored.shape[0]
    return stored.reshape(count, N_COL, -1, BLOCK).transpose(0, 2, 1, 3).reshape(count, -1)

def to_stored(logical):
    count = logical.shape[0]
    return logical.reshape(count, -1, N_COL, BLOCK).transpose(0, 2, 1, 3).reshape(count, -1)

def reference(slab):
    state = to_logical(slab)
    row_ids = jnp.arange(state.shape[0], dtype=jnp.int32)
    identity = jnp.eye(BLOCK, dtype=jnp.float32)
    for sub_step in range(2 * PANELS):
        start = sub_step * BLOCK
        stop = start + BLOCK
        diag_tile = state[start:stop, start:stop]
        lower_factor = jnp.linalg.cholesky(diag_tile)
        inverse = jax.scipy.linalg.solve_triangular(lower_factor, identity, lower=True)
        column = jnp.dot(state[:, start:stop].astype(jnp.float32), inverse.T.astype(jnp.float32), precision=PRECISE, preferred_element_type=jnp.float32)
        column = jnp.where(row_ids[:, None] < start, jnp.float32(0.0), column)
        column = column.at[start:stop].set(lower_factor)
        state = state.at[:, start:stop].set(column)
        if sub_step % 2 == 0:
            following = state[:, stop:stop + BLOCK] - jnp.dot(column.astype(jnp.float32), column[stop:stop + BLOCK].T.astype(jnp.float32), precision=PRECISE, preferred_element_type=jnp.float32)
            state = state.at[:, stop:stop + BLOCK].set(following)
        else:
            panel_left = state[:, start - BLOCK:stop]
            remaining = state[:, stop:]
            updated = remaining - jnp.dot(panel_left.astype(jnp.float32), panel_left[stop:SLAB_COLS].T.astype(jnp.float32), precision=PRECISE, preferred_element_type=jnp.float32)
            updated = jnp.where(row_ids[:, None] >= stop, updated, remaining)
            state = state.at[:, stop:].set(updated)
    return to_stored(state)
```

```python
import functools

import jax
import jax.numpy as jnp
from jax import lax
from jax.experimental import pallas as pl
from jax.experimental.pallas import tpu as pltpu
from jax.sharding import PartitionSpec as P

BLOCK = 256
PANELS = 2
LEAF = 128
SUB = 8
HEAD_BLOCKS = 2 * PANELS
HEAD = HEAD_BLOCKS * BLOCK
NT = (((1,), (1,)), ((), ()))
NN = (((1,), (0,)), ((), ()))


def exact(left_side, right_side, dims=NT):
    return lax.dot_general(left_side, right_side, dims, precision=lax.Precision.HIGHEST, preferred_element_type=jnp.float32)


def split(value):
    high = value.astype(jnp.bfloat16)
    low = (value - high.astype(jnp.float32)).astype(jnp.bfloat16)
    return high, low


def three(left_side, right_side):
    def dot(a, b):
        return lax.dot_general(a, b, NT, preferred_element_type=jnp.float32)
    return dot(left_side[0], right_side[1]) + dot(left_side[1], right_side[0]) + dot(left_side[0], right_side[0])


def lane(value, index):
    return jnp.broadcast_to(value[:, index : index + 1], (SUB, LEAF))


def sublane(value, index):
    return jnp.broadcast_to(value[index : index + 1, :], (SUB, LEAF))


def leaf(block):
    groups = LEAF // SUB
    rows = lax.broadcasted_iota(jnp.int32, (SUB, LEAF), 0)
    cols = lax.broadcasted_iota(jnp.int32, (SUB, LEAF), 1)
    left = [block[SUB * g : SUB * g + SUB, :] for g in range(groups)]
    right = [jnp.where(cols == rows + SUB * g, 1.0, 0.0).astype(jnp.float32) for g in range(groups)]
    upper, inverse = [], []
    for p in range(groups):
        columns = [lane(left[p], SUB * p + j) for j in range(SUB)]
        here_left, here_right = left[p], right[p]
        pivots, rows_left, rows_right, heads = [], [], [], []
        scale = jnp.zeros((SUB, LEAF), jnp.float32)
        for j in range(SUB):
            root = lax.rsqrt(sublane(columns[j], j))
            pivot = root * root
            scale = jnp.where(rows == j, root, scale)
            factor = jnp.where(rows > j, columns[j] * pivot, 0.0)
            row_left, row_right = sublane(here_left, j), sublane(here_right, j)
            head = {l: sublane(columns[l], j) for l in range(j + 1, SUB)}
            for l in range(j + 1, SUB):
                columns[l] = columns[l] - factor * head[l]
            here_left = here_left - factor * row_left
            here_right = here_right - factor * row_right
            pivots.append(pivot)
            rows_left.append(row_left)
            rows_right.append(row_right)
            heads.append(head)
        upper.append(jnp.where(cols >= rows + SUB * p, here_left * scale, 0.0))
        inverse.append(here_right * scale)
        for g in range(p + 1, groups):
            columns = [lane(left[g], SUB * p + j) for j in range(SUB)]
            for j in range(SUB):
                factor = columns[j] * pivots[j]
                for l in range(j + 1, SUB):
                    columns[l] = columns[l] - factor * heads[j][l]
                left[g] = left[g] - factor * rows_left[j]
                right[g] = right[g] - factor * rows_right[j]
    return jnp.concatenate(upper, 0), jnp.concatenate(inverse, 0)


def head_row_kernel(index, *refs):
    raw_ref = refs[0]
    above = refs[1 : 1 + index]
    inverses = refs[1 + index : 1 + 2 * index]
    row_ref, inverse_ref, work = refs[1 + 2 * index :]
    here = slice(index * BLOCK, (index + 1) * BLOCK)
    diagonal = raw_ref[:, here]
    for b in range(index):
        block = raw_ref[:, b * BLOCK : (b + 1) * BLOCK]
        if b:
            block = block - exact(row_ref[:, : b * BLOCK], above[b][:, : b * BLOCK])
        row_ref[:, b * BLOCK : (b + 1) * BLOCK] = exact(block, inverses[b][...])
    if index:
        solved = row_ref[:, : index * BLOCK]
        diagonal = diagonal - exact(solved, solved)
    work[...] = diagonal
    row_ref[:, here] = jnp.zeros((BLOCK, BLOCK), jnp.float32)
    inverse_ref[...] = jnp.zeros((BLOCK, BLOCK), jnp.float32)
    start = index * BLOCK

    def step(i, carry):
        place = pl.ds(pl.multiple_of(i * LEAF, LEAF), LEAF)
        upper, inverse = leaf(work[place, place])
        row_ref[place, pl.ds(pl.multiple_of(start + i * LEAF, LEAF), LEAF)] = upper.T
        inverse_ref[place, place] = inverse

        @pl.when(i == 0)
        def _():
            below = exact(work[LEAF:, :LEAF], inverse)
            row_ref[LEAF:, start : start + LEAF] = below
            work[LEAF:, LEAF:] = work[LEAF:, LEAF:] - exact(below, below)
            work[LEAF:, :LEAF] = exact(below, inverse, NN)

        @pl.when(i == 1)
        def _():
            inverse_ref[LEAF:, :LEAF] = -exact(inverse, work[LEAF:, :LEAF], NN)

        return carry

    lax.fori_loop(0, BLOCK // LEAF, step, 0)


def head_row(index, raw, above, inverses):
    return pl.pallas_call(
        functools.partial(head_row_kernel, index),
        out_shape=[
            jax.ShapeDtypeStruct((BLOCK, (index + 1) * BLOCK), jnp.float32),
            jax.ShapeDtypeStruct((BLOCK, BLOCK), jnp.float32),
        ],
        scratch_shapes=[pltpu.VMEM((BLOCK, BLOCK), jnp.float32)],
        compiler_params=pltpu.CompilerParams(vmem_limit_bytes=24 * 2**20),
        cost_estimate=pl.CostEstimate(flops=10_000_000_000, bytes_accessed=2**20, transcendentals=0),
        name=f"head_row_{index}",
    )(raw, *above, *inverses)


def finish_kernel(first_slot, col_count, place_ref, own_ref, mirror_ref, slab_ref, *refs):
    factor_rows = refs[:HEAD_BLOCKS]
    inverses = refs[HEAD_BLOCKS : 2 * HEAD_BLOCKS]
    out_ref, high_ref, low_ref = refs[2 * HEAD_BLOCKS :]
    row_count, width = slab_ref.shape
    first_row_block = place_ref[0] * (row_count // BLOCK)
    col_index = place_ref[1]
    mirror_rows = mirror_ref.shape[0]
    row_splits = [split(factor_rows[b][:, : b * BLOCK]) if b else None for b in range(HEAD_BLOCKS)]
    inverse_splits = [split(inverses[b][...]) for b in range(HEAD_BLOCKS)]
    out_ref[...] = slab_ref[...]

    def solve(rows, source_ref, source_rows, row_block):
        for b in range(HEAD_BLOCKS):
            here = slice(b * BLOCK, (b + 1) * BLOCK)
            value = source_ref[source_rows, here]
            if b:
                done = slice(0, b * BLOCK)
                value = value - three((high_ref[rows, done], low_ref[rows, done]), row_splits[b])
            solved = three(split(value), inverse_splits[b])
            kept = solved
            if row_block is not None:
                in_factor = jnp.where(row_block == b, factor_rows[b][:, here], jnp.where(row_block < b, 0.0, solved))
                slot = b // col_count

                @pl.when(col_index == b % col_count)
                def _():
                    out_ref[source_rows, slot * BLOCK : (slot + 1) * BLOCK] = in_factor

            high, low = split(kept)
            high_ref[rows, here] = high
            low_ref[rows, here] = low

    def own_tile(i, carry):
        place = pl.ds(pl.multiple_of(i * BLOCK, BLOCK), BLOCK)
        solve(place, own_ref, place, first_row_block + i)
        return carry

    def mirror_tile(i, carry):
        place = pl.ds(pl.multiple_of(row_count + i * BLOCK, BLOCK), BLOCK)
        solve(place, mirror_ref, pl.ds(pl.multiple_of(i * BLOCK, BLOCK), BLOCK), None)
        return carry

    lax.fori_loop(0, row_count // BLOCK, own_tile, 0)
    lax.fori_loop(0, mirror_rows // BLOCK, mirror_tile, 0)
    panel = 2 * BLOCK
    for i in range(row_count // BLOCK):
        rows = slice(i * BLOCK, (i + 1) * BLOCK)
        for k in range(first_slot, width // BLOCK):
            other = slice(row_count + (k - first_slot) * BLOCK, row_count + (k - first_slot + 1) * BLOCK)
            here = slice(k * BLOCK, (k + 1) * BLOCK)
            trailing = k * col_count + col_index >= HEAD_BLOCKS
            for count in range(1, PANELS + 1):
                done = slice(0, count * panel)
                block = first_row_block + i
                reached = block >= 2 * count
                if count < PANELS:
                    reached = reached & (block < 2 * count + 2)

                @pl.when(reached & trailing)
                def _():
                    change = three((high_ref[rows, done], low_ref[rows, done]), (high_ref[other, done], low_ref[other, done]))
                    out_ref[rows, here] = slab_ref[rows, here] - change


def finish(first_slot, col_count, place, own, mirror, slab, factor_rows, inverses):
    vmem = pl.BlockSpec(memory_space=pltpu.VMEM)
    rows = own.shape[0] + mirror.shape[0]
    return pl.pallas_call(
        functools.partial(finish_kernel, first_slot, col_count),
        out_shape=jax.ShapeDtypeStruct(slab.shape, jnp.float32),
        in_specs=[pl.BlockSpec(memory_space=pltpu.SMEM)] + [vmem] * (3 + 2 * HEAD_BLOCKS),
        out_specs=vmem,
        scratch_shapes=[pltpu.VMEM((rows, HEAD), jnp.bfloat16)] * 2,
        compiler_params=pltpu.CompilerParams(vmem_limit_bytes=48 * 2**20),
        cost_estimate=pl.CostEstimate(flops=20_000_000_000, bytes_accessed=2**23, transcendentals=0),
        name="finish",
    )(place, own, mirror, slab, *factor_rows, *inverses)


def gathered(slab):
    row_count, width = slab.shape
    col_count = lax.axis_size("col")
    owners = min(col_count, HEAD_BLOCKS)
    slots = HEAD_BLOCKS // owners
    first_slot = HEAD_BLOCKS // col_count
    own = lax.all_gather(slab[:, : slots * BLOCK], "col")[:owners]
    own = own.reshape(owners, row_count, slots, BLOCK).transpose(1, 2, 0, 3).reshape(row_count, HEAD)
    head_devices = HEAD // row_count
    head = lax.all_gather(own, "row")[:head_devices].reshape(HEAD, HEAD)
    mirror = lax.all_gather(slab[:, first_slot * BLOCK :], "row")[:head_devices]
    mirror = mirror.reshape(HEAD, width - first_slot * BLOCK).T
    raw = [head[b * BLOCK : (b + 1) * BLOCK, : (b + 1) * BLOCK] for b in range(HEAD_BLOCKS)]
    return raw, own, mirror


def exchanged(slab):
    row_count, width = slab.shape
    col_count = lax.axis_size("col")
    cores = 2
    ys = col_count // cores
    xs = ys
    zs = lax.axis_size("row") // xs
    r, c = lax.axis_index("row"), lax.axis_index("col")
    z, x, y, core = r // xs, r % xs, c // cores, c % cores
    tile = slab[:, :BLOCK]

    def flat(z, x, y, core):
        return (z * xs + x) * col_count + y * cores + core

    def send(value, pairs):
        return lax.ppermute(value, ("row", "col"), [(flat(*a), flat(*b)) for a, b in pairs])

    def plane(level=None):
        return [(a, b) for a in range(xs) for b in range(ys)]

    everyone = [(k, a, b, e) for k in range(zs) for a, b in plane() for e in range(cores)]

    def swap_core(value):
        return send(value, [((k, a, b, e), (k, a, b, 1 - e)) for k, a, b, e in everyone])

    def down(value):
        copies = [send(value, [((0, a, b, e), (k, a, b, e)) for a, b in plane() for e in range(cores)]) for k in range(1, zs)]
        return jnp.where(z == 0, value, sum(copies[1:], copies[0]))

    def across(value):
        flips = {}
        for dx, dy in ((1, 0), (0, 1), (1, 1)):
            flips[dx, dy] = send(value, [((k, a, b, e), (k, a ^ dx, b ^ dy, e)) for k, a, b, e in everyone])
        flips[0, 0] = value
        found = {}
        for a, b in plane():
            at_x = [jnp.where(y == b, flips[dx, 0], flips[dx, 1]) for dx in (0, 1)]
            found[a, b] = jnp.where(x == a, at_x[0], at_x[1])
        return found

    half = BLOCK // 2
    lower = send(tile[BLOCK + half :], [((0, 0, 0, 0), (0, 0, 0, 1))])
    packed = jnp.where(
        core == 0,
        tile[: BLOCK + half],
        jnp.concatenate([tile[BLOCK:], lower], 0),
    )
    quarter = packed.shape[0] // (xs * ys)
    pieces = [packed[i * quarter : (i + 1) * quarter] for i in range(xs * ys)]
    mine = jnp.where((x == 0) & (y == 0), pieces[0], 0.0)
    for i, (a, b) in enumerate(plane()):
        if i:
            mine = mine + send(pieces[i], [((0, 0, 0, e), (0, a, b, e)) for e in range(cores)])
    first = across(down(mine))
    first = jnp.concatenate([first[spot] for spot in plane()], 0)
    second = swap_core(first)
    zero, one = jnp.where(core == 0, first, second), jnp.where(core == 0, second, first)
    raw = [zero[:BLOCK], jnp.concatenate([jnp.concatenate([zero[BLOCK:], one[BLOCK:]], 0), one[:BLOCK]], 1)]
    upper = send(tile[:BLOCK], [((0, 1, b, e), (0, 0, b, e)) for b in range(ys) for e in range(cores)])
    rest = across(down(jnp.where(x == 0, upper, tile[BLOCK:])))
    for a in range(xs):
        pair = jnp.concatenate([rest[a, b] for b in range(ys)], 0)
        other = swap_core(pair)
        even, odd = jnp.where(core == 0, pair, other), jnp.where(core == 0, other, pair)
        blocks = [block[b * BLOCK : (b + 1) * BLOCK] for b in range(ys) for block in (even, odd)]
        raw.append(jnp.concatenate(blocks[: 3 + a], 1))
    own = lax.all_gather(tile, "col")
    own = own.transpose(1, 0, 2).reshape(row_count, HEAD)
    turned = send(tile, [((k, a, 1 - a, e), (k, 1 - a, a, e)) for k in range(1, zs) for a in range(xs) for e in range(cores)])
    part = jnp.where(x == y, tile, turned)
    steps = zs - 1
    held = [part]
    for shift in range(1, steps):
        held.append(
            send(part, [((1 + k, a, b, e), (1 + (k + shift) % steps, a, b, e)) for k in range(steps) for a, b in plane() for e in range(cores)])
        )
    ordered = []
    for k in range(1, zs):
        chosen = held[0]
        for shift in range(1, steps):
            chosen = jnp.where((z - k) % steps == shift, held[shift], chosen)
        ordered.append(chosen)
    ordered = jnp.stack(ordered, 0)
    keep = jnp.where(core == 0, ordered[:, :BLOCK], ordered[:, BLOCK:])
    give = jnp.where(core == 0, ordered[:, BLOCK:], ordered[:, :BLOCK])
    got = swap_core(give)
    wide = jnp.where(core == 0, jnp.concatenate([keep, got], 2), jnp.concatenate([got, keep], 2))
    straight = slab[:, BLOCK:].T.reshape(steps, BLOCK, row_count)
    wide = jnp.where(z == 0, straight, wide)
    over = send(wide, [((k, a, b, e), (k, 1 - a, b, e)) for k, a, b, e in everyone])
    mirror = jnp.where(x == 0, jnp.concatenate([wide, over], 2), jnp.concatenate([over, wide], 2))
    return raw, own, mirror.reshape(steps * BLOCK, HEAD)


def shards(slab):
    row_count, width = slab.shape
    row_total, col_count = lax.axis_size("row"), lax.axis_size("col")
    slots = width // BLOCK
    fits = (
        row_count == 2 * BLOCK
        and col_count == HEAD_BLOCKS
        and slots > 1
        and row_total == (col_count // 2) * slots
    )
    raw, own, mirror = exchanged(slab) if fits else gathered(slab)
    factor_rows, inverses = [], []
    for b in range(HEAD_BLOCKS):
        row, inverse = head_row(b, raw[b], factor_rows, inverses)
        factor_rows.append(row)
        inverses.append(inverse)
    place = jnp.stack([lax.axis_index("row"), lax.axis_index("col")]).astype(jnp.int32)
    return finish(HEAD_BLOCKS // col_count, col_count, place, own, mirror, slab, factor_rows, inverses)


def solution(mesh):
    in_specs = (P("row", "col"),)
    out_specs = P("row", "col")
    return jax.shard_map(shards, mesh=mesh, in_specs=in_specs, out_specs=out_specs, check_vma=False)
```

```python
import functools

import jax
import jax.numpy as jnp
from jax import lax
from jax.experimental import pallas as pl
from jax.experimental.pallas import tpu as pltpu
from jax.sharding import PartitionSpec as P

BLOCK = 256
PANELS = 2
LEAF = 128
SUB = 8
HEAD_BLOCKS = 2 * PANELS
HEAD = HEAD_BLOCKS * BLOCK
HEAD_COST = 10_000_000_000
NT = (((1,), (1,)), ((), ()))
NN = (((1,), (0,)), ((), ()))


def exact(left_side, right_side, dims=NT):
    return lax.dot_general(left_side, right_side, dims, precision=lax.Precision.HIGHEST, preferred_element_type=jnp.float32)


def split(value):
    high = value.astype(jnp.bfloat16)
    low = (value - high.astype(jnp.float32)).astype(jnp.bfloat16)
    return high, low


def three(left_side, right_side):
    def dot(a, b):
        return lax.dot_general(a, b, NT, preferred_element_type=jnp.float32)
    return dot(left_side[0], right_side[1]) + dot(left_side[1], right_side[0]) + dot(left_side[0], right_side[0])


def lane(value, index):
    return jnp.broadcast_to(value[:, index : index + 1], (SUB, LEAF))


def sublane(value, index):
    return jnp.broadcast_to(value[index : index + 1, :], (SUB, LEAF))


def leaf(block):
    groups = LEAF // SUB
    rows = lax.broadcasted_iota(jnp.int32, (SUB, LEAF), 0)
    cols = lax.broadcasted_iota(jnp.int32, (SUB, LEAF), 1)
    left = [block[SUB * g : SUB * g + SUB, :] for g in range(groups)]
    right = [jnp.where(cols == rows + SUB * g, 1.0, 0.0).astype(jnp.float32) for g in range(groups)]
    upper, inverse = [], []
    for p in range(groups):
        columns = [lane(left[p], SUB * p + j) for j in range(SUB)]
        here_left, here_right = left[p], right[p]
        pivots, rows_left, rows_right, heads = [], [], [], []
        scale = jnp.zeros((SUB, LEAF), jnp.float32)
        for j in range(SUB):
            root = lax.rsqrt(sublane(columns[j], j))
            pivot = root * root
            scale = jnp.where(rows == j, root, scale)
            below = jnp.where(rows > j, columns[j], 0.0)
            factor = below * pivot
            row_left, row_right = sublane(here_left, j), sublane(here_right, j)
            head = {l: sublane(columns[l], j) for l in range(j + 1, SUB)}
            if j + 1 < SUB:
                columns[j + 1] = columns[j + 1] - (below * root) * (head[j + 1] * root)
            for l in range(j + 2, SUB):
                columns[l] = columns[l] - factor * head[l]
            here_left = here_left - factor * row_left
            here_right = here_right - factor * row_right
            pivots.append(pivot)
            rows_left.append(row_left)
            rows_right.append(row_right)
            heads.append(head)
        upper.append(jnp.where(cols >= rows + SUB * p, here_left * scale, 0.0))
        inverse.append(here_right * scale)
        for g in range(p + 1, groups):
            columns = [lane(left[g], SUB * p + j) for j in range(SUB)]
            for j in range(SUB):
                factor = columns[j] * pivots[j]
                for l in range(j + 1, SUB):
                    columns[l] = columns[l] - factor * heads[j][l]
                left[g] = left[g] - factor * rows_left[j]
                right[g] = right[g] - factor * rows_right[j]
    return jnp.concatenate(upper, 0), jnp.concatenate(inverse, 0)


def head_row_kernel(index, fetch, pieces, ready, place_ref, *refs):
    raw = refs[:pieces]
    above = refs[pieces : pieces + index]
    inverses = refs[pieces + index : pieces + 2 * index]
    row_ref, inverse_ref, work = refs[pieces + 2 * index + ready :]
    here = slice(index * BLOCK, (index + 1) * BLOCK)
    block_of = functools.partial(fetch, place_ref[0], place_ref[1], raw, index)
    for b in range(index):
        block = block_of(b)
        if b:
            block = block - exact(row_ref[:, : b * BLOCK], above[b][:, : b * BLOCK])
        row_ref[:, b * BLOCK : (b + 1) * BLOCK] = exact(block, inverses[b][...])
    diagonal = block_of(index)
    if index:
        solved = row_ref[:, : index * BLOCK]
        diagonal = diagonal - exact(solved, solved)
    work[...] = diagonal
    row_ref[:, here] = jnp.zeros((BLOCK, BLOCK), jnp.float32)
    inverse_ref[...] = jnp.zeros((BLOCK, BLOCK), jnp.float32)
    start = index * BLOCK

    def step(i, carry):
        place = pl.ds(pl.multiple_of(i * LEAF, LEAF), LEAF)
        upper, inverse = leaf(work[place, place])
        row_ref[place, pl.ds(pl.multiple_of(start + i * LEAF, LEAF), LEAF)] = upper.T
        inverse_ref[place, place] = inverse

        @pl.when(i == 0)
        def _():
            below = exact(work[LEAF:, :LEAF], inverse)
            row_ref[LEAF:, start : start + LEAF] = below
            work[LEAF:, LEAF:] = work[LEAF:, LEAF:] - exact(below, below)
            work[LEAF:, :LEAF] = exact(below, inverse, NN)

        @pl.when(i == 1)
        def _():
            inverse_ref[LEAF:, :LEAF] = -exact(inverse, work[LEAF:, :LEAF], NN)

        return carry

    lax.fori_loop(0, BLOCK // LEAF, step, 0)


def head_row(index, fetch, place, raw, ready, above, inverses):
    return pl.pallas_call(
        functools.partial(head_row_kernel, index, fetch, len(raw), len(ready)),
        out_shape=[
            jax.ShapeDtypeStruct((BLOCK, (index + 1) * BLOCK), jnp.float32),
            jax.ShapeDtypeStruct((BLOCK, BLOCK), jnp.float32),
        ],
        in_specs=[pl.BlockSpec(memory_space=pltpu.SMEM)] + [pl.BlockSpec(memory_space=pltpu.VMEM)] * (len(raw) + 2 * index)
        + [pl.BlockSpec(memory_space=pl.ANY)] * len(ready),
        scratch_shapes=[pltpu.VMEM((BLOCK, BLOCK), jnp.float32)],
        compiler_params=pltpu.CompilerParams(vmem_limit_bytes=24 * 2**20),
        cost_estimate=pl.CostEstimate(flops=HEAD_COST, bytes_accessed=2**20, transcendentals=0),
        name=f"head_row_{index}",
    )(place, *raw, *above, *inverses, *ready)


def solve(fetch, high_ref, low_ref, row_splits, inverse_splits, store=None):
    for b in range(HEAD_BLOCKS):
        here, done = slice(b * BLOCK, (b + 1) * BLOCK), slice(0, b * BLOCK)
        value = fetch(b)
        if b:
            value = value - three((high_ref[:, done], low_ref[:, done]), row_splits[b])
        solved = three(split(value), inverse_splits[b])
        if store is not None:
            store(b, solved)
        high, low = split(solved)
        high_ref[:, here] = high
        low_ref[:, here] = low


def own_kernel(col_count, fetch, owned, place_ref, slab_ref, *refs):
    own = refs[:owned]
    factor_rows = refs[owned : owned + HEAD_BLOCKS]
    inverses = refs[owned + HEAD_BLOCKS : owned + 2 * HEAD_BLOCKS]
    outs = refs[owned + 2 * HEAD_BLOCKS :]
    column_ref, high_ref, low_ref = outs[:3]
    row_refs, inverse_refs = outs[3 : 1 + 2 * HEAD_BLOCKS], outs[1 + 2 * HEAD_BLOCKS :]
    row_count = high_ref.shape[0]
    row_index, col_index = place_ref[0], place_ref[1]
    first_row_block = row_index * (row_count // BLOCK)
    column_ref[...] = slab_ref[:, : column_ref.shape[1]]
    row_splits, inverse_splits = [None], []
    for b in range(HEAD_BLOCKS):
        if b:
            row_splits.append(split(factor_rows[b][:, : b * BLOCK]))
            row_refs[2 * b - 2][...], row_refs[2 * b - 1][...] = row_splits[b]
        inverse_splits.append(split(inverses[b][...]))
        inverse_refs[2 * b][...], inverse_refs[2 * b + 1][...] = inverse_splits[b]

    def store(b, solved):
        slot = slice(b // col_count * BLOCK, (b // col_count + 1) * BLOCK)

        @pl.when(col_index == b % col_count)
        def _():
            diagonal = factor_rows[b][:, b * BLOCK : (b + 1) * BLOCK]
            for i in range(row_count // BLOCK):
                rows = slice(i * BLOCK, (i + 1) * BLOCK)
                block = first_row_block + i
                column_ref[rows, slot] = jnp.where(block == b, diagonal, jnp.where(block < b, 0.0, solved[rows]))

    solve(lambda b: fetch(row_index, col_index, own, b), high_ref, low_ref, row_splits, inverse_splits, store)


def mirror_kernel(first_slot, col_count, fetch, slot_of, pieces, place_ref, slab_ref, *refs):
    mirrored = refs[:pieces] + refs[-1:]
    column_ref, own_high, own_low = refs[pieces : pieces + 3]
    splits = refs[pieces + 3 : pieces + 1 + 4 * HEAD_BLOCKS]
    row_refs, inverse_refs = splits[: 2 * HEAD_BLOCKS - 2], splits[2 * HEAD_BLOCKS - 2 :]
    out_ref, state, high_ref, low_ref, raw_ref, into, outof, _ = refs[pieces + 1 + 4 * HEAD_BLOCKS :]
    row_count, width = slab_ref.shape
    row_index, col_index = place_ref[0], place_ref[1]
    first_row_block = row_index * (row_count // BLOCK)
    slots = range(width // BLOCK)
    arrive = [
        pltpu.make_async_copy(slab_ref.at[:, k * BLOCK : (k + 1) * BLOCK], state.at[:, k * BLOCK : (k + 1) * BLOCK], into.at[k])
        for k in slots
    ]
    leave = [
        pltpu.make_async_copy(state.at[:, k * BLOCK : (k + 1) * BLOCK], out_ref.at[:, k * BLOCK : (k + 1) * BLOCK], outof.at[k])
        for k in slots
    ]
    for copy in arrive:
        copy.start()
    count = width // BLOCK - first_slot
    places = [pl.ds(pl.multiple_of(slot_of(row_index, i) * BLOCK, BLOCK), BLOCK) for i in range(count)]

    def block_of(b):
        for i in range(count):
            raw_ref[places[i], :] = fetch(row_index, col_index, mirrored, i, b)
        return raw_ref[...]

    row_splits = [None] + [(row_refs[2 * b - 2][...], row_refs[2 * b - 1][...]) for b in range(1, HEAD_BLOCKS)]
    inverse_splits = [(inverse_refs[2 * b][...], inverse_refs[2 * b + 1][...]) for b in range(HEAD_BLOCKS)]
    solve(block_of, high_ref, low_ref, row_splits, inverse_splits)
    panel = 2 * BLOCK
    head_slots = column_ref.shape[1] // BLOCK
    for k in slots:
        arrive[k].wait()
        here = slice(k * BLOCK, (k + 1) * BLOCK)
        if k < head_slots:
            state[:, here] = column_ref[:, here]
        if k >= first_slot:
            other = slice((k - first_slot) * BLOCK, (k - first_slot + 1) * BLOCK)
            trailing = k * col_count + col_index >= HEAD_BLOCKS
            last = first_row_block >= HEAD_BLOCKS

            @pl.when(last & trailing)
            def _():
                change = three((own_high[...], own_low[...]), (high_ref[other, :], low_ref[other, :]))
                state[:, here] = state[:, here] - change

            for i in range(row_count // BLOCK):
                rows = slice(i * BLOCK, (i + 1) * BLOCK)
                for done in range(1, PANELS + 1):
                    inner = slice(0, done * panel)
                    block = first_row_block + i
                    reached = (block >= 2 * done) & (first_row_block < HEAD_BLOCKS)
                    if done < PANELS:
                        reached = reached & (block < 2 * done + 2)

                    @pl.when(reached & trailing)
                    def _():
                        change = three((own_high[rows, inner], own_low[rows, inner]), (high_ref[other, inner], low_ref[other, inner]))
                        state[rows, here] = state[rows, here] - change
        leave[k].start()
    for copy in leave:
        copy.wait()


def finish_own(col_count, fetch, place, slab, own, factor_rows, inverses):
    row_count = slab.shape[0]
    vmem = pl.BlockSpec(memory_space=pltpu.VMEM)
    head_width = -(-HEAD_BLOCKS // col_count) * BLOCK
    half = [jax.ShapeDtypeStruct((row_count, HEAD), jnp.bfloat16)] * 2
    rows = [jax.ShapeDtypeStruct((BLOCK, b * BLOCK), jnp.bfloat16) for b in range(1, HEAD_BLOCKS) for _ in range(2)]
    squares = [jax.ShapeDtypeStruct((BLOCK, BLOCK), jnp.bfloat16)] * (2 * HEAD_BLOCKS)
    return pl.pallas_call(
        functools.partial(own_kernel, col_count, fetch, len(own)),
        out_shape=[jax.ShapeDtypeStruct((row_count, head_width), jnp.float32)] + half + rows + squares,
        in_specs=[pl.BlockSpec(memory_space=pltpu.SMEM)] + [vmem] * (1 + len(own) + 2 * HEAD_BLOCKS),
        compiler_params=pltpu.CompilerParams(vmem_limit_bytes=32 * 2**20),
        cost_estimate=pl.CostEstimate(flops=8_000_000_000, bytes_accessed=2**20, transcendentals=0),
        name="finish_own",
    )(place, slab[:, :head_width], *own, *factor_rows, *inverses)


def finish_mirror(first_slot, col_count, fetch, slot_of, place, slab, mirrored, solved):
    vmem = pl.BlockSpec(memory_space=pltpu.VMEM)
    anywhere = pl.BlockSpec(memory_space=pl.ANY)
    row_count, width = slab.shape
    rows = width - first_slot * BLOCK
    return pl.pallas_call(
        functools.partial(mirror_kernel, first_slot, col_count, fetch, slot_of, len(mirrored)),
        out_shape=jax.ShapeDtypeStruct(slab.shape, jnp.float32),
        in_specs=[pl.BlockSpec(memory_space=pltpu.SMEM), anywhere] + [vmem] * (len(mirrored) + len(solved)),
        out_specs=anywhere,
        scratch_shapes=[
            pltpu.VMEM(slab.shape, jnp.float32),
            pltpu.VMEM((rows, HEAD), jnp.bfloat16),
            pltpu.VMEM((rows, HEAD), jnp.bfloat16),
            pltpu.VMEM((rows, BLOCK), jnp.float32),
            pltpu.SemaphoreType.DMA((width // BLOCK,)),
            pltpu.SemaphoreType.DMA((width // BLOCK,)),
            pltpu.VMEM((BLOCK, BLOCK), jnp.float32),
        ],
        compiler_params=pltpu.CompilerParams(vmem_limit_bytes=40 * 2**20),
        cost_estimate=pl.CostEstimate(flops=10_000_000_000, bytes_accessed=2**23, transcendentals=0),
        name="finish_mirror",
    )(place, slab, *mirrored, *solved)


def after(value, *tokens):
    return value + jnp.minimum(sum(jnp.abs(token[0, 0]) for token in tokens), 0.0)


def gathered(slab):
    row_count, width = slab.shape
    col_count = lax.axis_size("col")
    owners = min(col_count, HEAD_BLOCKS)
    slots = HEAD_BLOCKS // owners
    first_slot = HEAD_BLOCKS // col_count
    own = lax.all_gather(slab[:, : slots * BLOCK], "col")[:owners]
    own = own.reshape(owners, row_count, slots, BLOCK).transpose(2, 0, 1, 3).reshape(HEAD_BLOCKS, row_count, BLOCK)
    devices = HEAD // row_count
    head = lax.all_gather(own, "row")[:devices].transpose(0, 2, 1, 3).reshape(HEAD_BLOCKS, BLOCK, HEAD)
    mirror = lax.all_gather(slab[:, first_slot * BLOCK :], "row")[:devices]
    mirror = mirror.reshape(HEAD, width - first_slot * BLOCK).T.reshape(-1, BLOCK, HEAD)

    def head_block(row, col, refs, index, b):
        return refs[0][:, b * BLOCK : (b + 1) * BLOCK]

    def mirror_block(row, col, refs, i, b):
        return refs[0][i, :, b * BLOCK : (b + 1) * BLOCK]

    def own_block(row, col, refs, b):
        return refs[0][b]

    def raw(b, inverses):
        return [head[b]], []

    def complete(token):
        return [own], [mirror]

    return raw, [head_block] * HEAD_BLOCKS, complete, own_block, mirror_block, lambda row, i: i


def exchanged(slab):
    row_count, width = slab.shape
    col_count = lax.axis_size("col")
    cores = 2
    ys = col_count // cores
    xs = ys
    zs = lax.axis_size("row") // xs
    r, c = lax.axis_index("row"), lax.axis_index("col")
    z, x, y, core = r // xs, r % xs, c // cores, c % cores
    tile = slab[:, :BLOCK]
    top, bottom = tile[:BLOCK], tile[BLOCK:]
    spots = [(a, b, e) for a in range(xs) for b in range(ys) for e in range(cores)]
    everyone = [(k, *spot) for k in range(zs) for spot in spots]

    def flat(z, x, y, core):
        return (z * xs + x) * col_count + y * cores + core

    def send(value, pairs):
        return lax.ppermute(value, ("row", "col"), [(flat(*a), flat(*b)) for a, b in pairs])

    def swap_core(value):
        return send(value, [((k, a, b, e), (k, a, b, 1 - e)) for k, a, b, e in everyone])

    def swap_x(value):
        return send(value, [((k, a, b, e), (k, 1 - a, b, e)) for k, a, b, e in everyone])

    def swap_y(value):
        return send(value, [((k, a, b, e), (k, a, 1 - b, e)) for k, a, b, e in everyone])

    def down(value, sources, steps=None):
        stride = zs // 2
        have = [0]
        while stride:
            came = send(value, [((k, *s), (k + stride, *s)) for k in have for s in sources])
            value = jnp.where(functools.reduce(jnp.logical_or, [z == k for k in have]), value, came)
            have = have + [k + stride for k in have]
            stride //= 2
            if steps is not None:
                steps.append(value)
        return value

    def spread(value, sources):
        came = send(value, [((k, 0, 0, e), (k, 1, 0, e)) for k in range(zs) for e in sources])
        value = jnp.where(x == 0, value, came)
        came = send(value, [((k, a, 0, e), (k, a, 1, e)) for k in range(zs) for a in range(xs) for e in sources])
        return jnp.where(y == 0, value, came)

    zero_z = down(top, [(0, 0, 0)])
    zero_here = spread(zero_z, [0])
    zero = send(zero_here, [((k, a, b, 0), (k, a, b, 1)) for k, a, b, e in everyone if e == 0])
    zero = jnp.where(core == 0, zero_here, zero)
    one_here = spread(down(bottom, [(0, 0, 0), (0, 0, 1)]), [0, 1])
    rest_steps = []
    came = send(top, [((0, 1, b, e), (0, 0, b, e)) for b in range(ys) for e in range(cores)])
    rest_here = down(jnp.where(x == 0, after(came, zero_z), bottom), spots, rest_steps)
    steps = zs - 1
    turned = send(tile, [((k, a, 1 - a, e), (k, 1 - a, a, e)) for k in range(1, zs) for a in range(xs) for e in range(cores)])
    part = jnp.where(x == y, tile, after(turned, zero_here))
    passed = [part]
    for shift in range(1, steps):
        passed.append(
            send(part, [((1 + k, *s), (1 + (k + shift) % steps, *s)) for k in range(steps) for s in spots])
        )
    mirrored = []

    def mirror(shift, token):
        held = jnp.where(z == 0, slab[:, (1 + shift) * BLOCK : (2 + shift) * BLOCK], after(passed[shift], token))
        mirrored.append([held, swap_x(held)])

    kept = {}

    def raw(b, inverses):
        if b == 0:
            return [zero], [turned, rest_here]
        if b == 1:
            one = after(one_here, inverses[0])
            one_other = swap_core(one)
            flips = []
            mirror(0, zero_here)
            later = after(rest_here, one_other, passed[1], mirrored[0][1])
            for dx, dy in ((1, 1), (1, 0), (0, 1)):
                flips.append(send(later, [((k, i, j, e), (k, i ^ dx, j ^ dy, e)) for k, i, j, e in everyone]))
            kept["rest"] = [later, flips[1], flips[2], flips[0]]
            return [one, one_other], []
        if b == 2:
            rest = after(jnp.stack(kept["rest"], 0), inverses[1], *passed[2:])
            rest_other = swap_core(rest)
            kept["rest"] = [rest, rest_other]
            for shift in range(1, steps):
                mirror(shift, rest_other[0])
            kept["own"] = swap_y(after(tile, rest_other[0]))
            return kept["rest"], []
        return kept["rest"], []

    def complete(token):
        own = [tile, kept["own"], swap_core(tile), swap_core(kept["own"])]
        pieces = [value for pair in mirrored for value in pair]
        give = jnp.stack([jnp.where(core == 0, value[BLOCK:], value[:BLOCK]) for value in pieces], 0)
        return own, pieces + [swap_core(after(give, token))]

    def here(row, col):
        return row // xs, row % xs, col // cores, col % cores

    def first_block(row, col, refs, index, b):
        return refs[0][...]

    def second_block(row, col, refs, index, b):
        return jnp.where(here(row, col)[3] == b, refs[0][...], refs[1][...])

    def rest_block(row, col, refs, index, b):
        z, x, y, core = here(row, col)
        place = jnp.where(y == b // cores, 0, 2) + jnp.where(x == index - 2, 0, 1)
        return jnp.where(core == b % cores, refs[0][place], refs[1][place])

    def mirror_block(row, col, refs, i, b):
        z, x, y, core = here(row, col)
        got, stage = refs[2 * steps :]
        same_x = x == b // cores

        @pl.when(z == 0)
        def _():
            rows = slice((b % cores) * BLOCK, (b % cores + 1) * BLOCK)
            stage[...] = jnp.where(same_x, refs[2 * i][rows, :], refs[2 * i + 1][rows, :]).T

        @pl.when(z != 0)
        def _():
            rows = pl.ds(pl.multiple_of(core * BLOCK, BLOCK), BLOCK)
            near = jnp.where(same_x, refs[2 * i][rows, :], refs[2 * i + 1][rows, :])
            stage[...] = jnp.where(core == b % cores, near, got[2 * i + jnp.where(same_x, 0, 1)])

        return stage[...]

    def own_block(row, col, refs, b):
        z, x, y, core = here(row, col)
        same = jnp.where(y == b // cores, refs[0][...], refs[1][...])
        other = jnp.where(y == b // cores, refs[2][...], refs[3][...])
        return jnp.where(core == b % cores, same, other)

    def slot_of(row, i):
        z = row // xs
        return jnp.where(z == 0, i, lax.rem(z - 1 - i + steps, steps))

    fetch_mirror, fetch_own = mirror_block, own_block
    return raw, [first_block, second_block, rest_block, rest_block], complete, fetch_own, fetch_mirror, slot_of


def shards(slab):
    row_count, width = slab.shape
    row_total, col_count = lax.axis_size("row"), lax.axis_size("col")
    slots = width // BLOCK
    fits = (
        row_count == 2 * BLOCK
        and col_count == HEAD_BLOCKS
        and slots > 1
        and slots & (slots - 1) == 0
        and row_total == (col_count // 2) * slots
    )
    raw, fetch, complete, own_fetch, mirror_fetch, slot_of = exchanged(slab) if fits else gathered(slab)
    place = jnp.stack([lax.axis_index("row"), lax.axis_index("col")]).astype(jnp.int32)
    factor_rows, inverses = [], []
    for b in range(HEAD_BLOCKS):
        pieces, ready = raw(b, inverses)
        row, inverse = head_row(b, fetch[b], place, pieces, ready, factor_rows, inverses)
        factor_rows.append(row)
        inverses.append(inverse)
    own, mirrored = complete(inverses[-1])
    solved = finish_own(col_count, own_fetch, place, slab, own, factor_rows, inverses)
    return finish_mirror(HEAD_BLOCKS // col_count, col_count, mirror_fetch, slot_of, place, slab, mirrored, solved)


def solution(mesh):
    in_specs = (P("row", "col"),)
    out_specs = P("row", "col")
    return jax.shard_map(shards, mesh=mesh, in_specs=in_specs, out_specs=out_specs, check_vma=False)
```

```python
import functools

import jax
import jax.numpy as jnp
from jax import lax
from jax.experimental import pallas as pl
from jax.experimental.pallas import tpu as pltpu
from jax.sharding import PartitionSpec as P

BLOCK = 256
PANELS = 2
LEAF = 128
SUB = 8
HEAD_BLOCKS = 2 * PANELS
HEAD = HEAD_BLOCKS * BLOCK
HEAD_COST = 10_000_000_000
NT = (((1,), (1,)), ((), ()))
NN = (((1,), (0,)), ((), ()))


def exact(left_side, right_side, dims=NT):
    return lax.dot_general(left_side, right_side, dims, precision=lax.Precision.HIGHEST, preferred_element_type=jnp.float32)


def split(value):
    high = value.astype(jnp.bfloat16)
    low = (value - high.astype(jnp.float32)).astype(jnp.bfloat16)
    return high, low


def three(left_side, right_side):
    def dot(a, b):
        return lax.dot_general(a, b, NT, preferred_element_type=jnp.float32)
    return dot(left_side[0], right_side[1]) + dot(left_side[1], right_side[0]) + dot(left_side[0], right_side[0])


def lane(value, index):
    return jnp.broadcast_to(value[:, index : index + 1], (SUB, LEAF))


def sublane(value, index):
    return jnp.broadcast_to(value[index : index + 1, :], (SUB, LEAF))


def leaf(block):
    groups = LEAF // SUB
    rows = lax.broadcasted_iota(jnp.int32, (SUB, LEAF), 0)
    cols = lax.broadcasted_iota(jnp.int32, (SUB, LEAF), 1)
    left = [block[SUB * g : SUB * g + SUB, :] for g in range(groups)]
    right = [jnp.where(cols == rows + SUB * g, 1.0, 0.0).astype(jnp.float32) for g in range(groups)]
    upper, inverse = [], []
    for p in range(groups):
        columns = [lane(left[p], SUB * p + j) for j in range(SUB)]
        here_left, here_right = left[p], right[p]
        pivots, rows_left, rows_right, heads = [], [], [], []
        scale = jnp.zeros((SUB, LEAF), jnp.float32)
        for j in range(SUB):
            root = lax.rsqrt(sublane(columns[j], j))
            pivot = root * root
            scale = jnp.where(rows == j, root, scale)
            below = jnp.where(rows > j, columns[j], 0.0)
            factor = below * pivot
            row_left, row_right = sublane(here_left, j), sublane(here_right, j)
            head = {l: sublane(columns[l], j) for l in range(j + 1, SUB)}
            if j + 1 < SUB:
                columns[j + 1] = columns[j + 1] - (below * root) * (head[j + 1] * root)
            for l in range(j + 2, SUB):
                columns[l] = columns[l] - factor * head[l]
            here_left = here_left - factor * row_left
            here_right = here_right - factor * row_right
            pivots.append(pivot)
            rows_left.append(row_left)
            rows_right.append(row_right)
            heads.append(head)
        upper.append(jnp.where(cols >= rows + SUB * p, here_left * scale, 0.0))
        inverse.append(here_right * scale)
        for g in range(p + 1, groups):
            columns = [lane(left[g], SUB * p + j) for j in range(SUB)]
            for j in range(SUB):
                factor = columns[j] * pivots[j]
                for l in range(j + 1, SUB):
                    columns[l] = columns[l] - factor * heads[j][l]
                left[g] = left[g] - factor * rows_left[j]
                right[g] = right[g] - factor * rows_right[j]
    return jnp.concatenate(upper, 0), jnp.concatenate(inverse, 0)


def head_row_kernel(index, fetch, pieces, ready, place_ref, *refs):
    raw = refs[:pieces]
    above = refs[pieces : pieces + index]
    inverses = refs[pieces + index : pieces + 2 * index]
    row_ref, inverse_ref, work = refs[pieces + 2 * index + ready :]
    here = slice(index * BLOCK, (index + 1) * BLOCK)
    block_of = functools.partial(fetch, place_ref[0], place_ref[1], raw, index)
    for b in range(index):
        block = block_of(b)
        if b:
            block = block - exact(row_ref[:, : b * BLOCK], above[b][:, : b * BLOCK])
        row_ref[:, b * BLOCK : (b + 1) * BLOCK] = exact(block, inverses[b][...])
    diagonal = block_of(index)
    if index:
        solved = row_ref[:, : index * BLOCK]
        diagonal = diagonal - exact(solved, solved)
    work[...] = diagonal
    row_ref[:, here] = jnp.zeros((BLOCK, BLOCK), jnp.float32)
    inverse_ref[...] = jnp.zeros((BLOCK, BLOCK), jnp.float32)
    start = index * BLOCK

    def step(i, carry):
        place = pl.ds(pl.multiple_of(i * LEAF, LEAF), LEAF)
        upper, inverse = leaf(work[place, place])
        row_ref[place, pl.ds(pl.multiple_of(start + i * LEAF, LEAF), LEAF)] = upper.T
        inverse_ref[place, place] = inverse

        @pl.when(i == 0)
        def _():
            below = exact(work[LEAF:, :LEAF], inverse)
            row_ref[LEAF:, start : start + LEAF] = below
            work[LEAF:, LEAF:] = work[LEAF:, LEAF:] - exact(below, below)
            work[LEAF:, :LEAF] = exact(below, inverse, NN)

        @pl.when(i == 1)
        def _():
            inverse_ref[LEAF:, :LEAF] = -exact(inverse, work[LEAF:, :LEAF], NN)

        return carry

    lax.fori_loop(0, BLOCK // LEAF, step, 0)


def head_row(index, fetch, place, raw, ready, above, inverses):
    return pl.pallas_call(
        functools.partial(head_row_kernel, index, fetch, len(raw), len(ready)),
        out_shape=[
            jax.ShapeDtypeStruct((BLOCK, (index + 1) * BLOCK), jnp.float32),
            jax.ShapeDtypeStruct((BLOCK, BLOCK), jnp.float32),
        ],
        in_specs=[pl.BlockSpec(memory_space=pltpu.SMEM)] + [pl.BlockSpec(memory_space=pltpu.VMEM)] * (len(raw) + 2 * index)
        + [pl.BlockSpec(memory_space=pl.ANY)] * len(ready),
        scratch_shapes=[pltpu.VMEM((BLOCK, BLOCK), jnp.float32)],
        compiler_params=pltpu.CompilerParams(vmem_limit_bytes=24 * 2**20),
        cost_estimate=pl.CostEstimate(flops=HEAD_COST, bytes_accessed=2**20, transcendentals=0),
        name=f"head_row_{index}",
    )(place, *raw, *above, *inverses, *ready)


def solve(fetch, high_ref, low_ref, row_splits, inverse_splits, store=None):
    for b in range(HEAD_BLOCKS):
        here, done = slice(b * BLOCK, (b + 1) * BLOCK), slice(0, b * BLOCK)
        value = fetch(b)
        if b:
            value = value - three((high_ref[:, done], low_ref[:, done]), row_splits[b])
        solved = three(split(value), inverse_splits[b])
        if store is not None:
            store(b, solved)
        high, low = split(solved)
        high_ref[:, here] = high
        low_ref[:, here] = low


def own_kernel(col_count, fetch, owned, place_ref, slab_ref, *refs):
    own = refs[:owned]
    factor_rows = refs[owned : owned + HEAD_BLOCKS]
    inverses = refs[owned + HEAD_BLOCKS : owned + 2 * HEAD_BLOCKS]
    outs = refs[owned + 2 * HEAD_BLOCKS :]
    column_ref, high_ref, low_ref = outs[:3]
    row_refs, inverse_refs = outs[3 : 1 + 2 * HEAD_BLOCKS], outs[1 + 2 * HEAD_BLOCKS :]
    row_count = high_ref.shape[0]
    row_index, col_index = place_ref[0], place_ref[1]
    first_row_block = row_index * (row_count // BLOCK)
    column_ref[...] = slab_ref[:, : column_ref.shape[1]]
    row_splits, inverse_splits = [None], []
    for b in range(HEAD_BLOCKS):
        if b:
            row_splits.append(split(factor_rows[b][:, : b * BLOCK]))
            row_refs[2 * b - 2][...], row_refs[2 * b - 1][...] = row_splits[b]
        inverse_splits.append(split(inverses[b][...]))
        inverse_refs[2 * b][...], inverse_refs[2 * b + 1][...] = inverse_splits[b]

    def store(b, solved):
        slot = slice(b // col_count * BLOCK, (b // col_count + 1) * BLOCK)

        @pl.when(col_index == b % col_count)
        def _():
            diagonal = factor_rows[b][:, b * BLOCK : (b + 1) * BLOCK]
            for i in range(row_count // BLOCK):
                rows = slice(i * BLOCK, (i + 1) * BLOCK)
                block = first_row_block + i
                column_ref[rows, slot] = jnp.where(block == b, diagonal, jnp.where(block < b, 0.0, solved[rows]))

    solve(lambda b: fetch(row_index, col_index, own, b), high_ref, low_ref, row_splits, inverse_splits, store)


def mirror_kernel(first_slot, col_count, fetch, slot_of, pieces, place_ref, slab_ref, *refs):
    mirrored = refs[:pieces] + refs[-1:]
    column_ref, own_high, own_low = refs[pieces : pieces + 3]
    splits = refs[pieces + 3 : pieces + 1 + 4 * HEAD_BLOCKS]
    row_refs, inverse_refs = splits[: 2 * HEAD_BLOCKS - 2], splits[2 * HEAD_BLOCKS - 2 :]
    out_ref, state, high_ref, low_ref, raw_ref, into, outof, _ = refs[pieces + 1 + 4 * HEAD_BLOCKS :]
    row_count, width = slab_ref.shape
    row_index, col_index = place_ref[0], place_ref[1]
    first_row_block = row_index * (row_count // BLOCK)
    slots = range(width // BLOCK)
    arrive = [
        pltpu.make_async_copy(slab_ref.at[:, k * BLOCK : (k + 1) * BLOCK], state.at[:, k * BLOCK : (k + 1) * BLOCK], into.at[k])
        for k in slots
    ]
    leave = [
        pltpu.make_async_copy(state.at[:, k * BLOCK : (k + 1) * BLOCK], out_ref.at[:, k * BLOCK : (k + 1) * BLOCK], outof.at[k])
        for k in slots
    ]
    for copy in arrive:
        copy.start()
    count = width // BLOCK - first_slot
    places = [pl.ds(pl.multiple_of(slot_of(row_index, i) * BLOCK, BLOCK), BLOCK) for i in range(count)]

    def block_of(b):
        for i in range(count):
            raw_ref[places[i], :] = fetch(row_index, col_index, mirrored, i, b)
        return raw_ref[...]

    row_splits = [None] + [(row_refs[2 * b - 2][...], row_refs[2 * b - 1][...]) for b in range(1, HEAD_BLOCKS)]
    inverse_splits = [(inverse_refs[2 * b][...], inverse_refs[2 * b + 1][...]) for b in range(HEAD_BLOCKS)]
    solve(block_of, high_ref, low_ref, row_splits, inverse_splits)
    panel = 2 * BLOCK
    head_slots = column_ref.shape[1] // BLOCK
    for k in slots:
        arrive[k].wait()
        here = slice(k * BLOCK, (k + 1) * BLOCK)
        if k < head_slots:
            state[:, here] = column_ref[:, here]
        if k >= first_slot:
            other = slice((k - first_slot) * BLOCK, (k - first_slot + 1) * BLOCK)
            trailing = k * col_count + col_index >= HEAD_BLOCKS
            last = first_row_block >= HEAD_BLOCKS

            @pl.when(last & trailing)
            def _():
                change = three((own_high[...], own_low[...]), (high_ref[other, :], low_ref[other, :]))
                state[:, here] = state[:, here] - change

            for i in range(row_count // BLOCK):
                rows = slice(i * BLOCK, (i + 1) * BLOCK)
                for done in range(1, PANELS + 1):
                    inner = slice(0, done * panel)
                    block = first_row_block + i
                    reached = (block >= 2 * done) & (first_row_block < HEAD_BLOCKS)
                    if done < PANELS:
                        reached = reached & (block < 2 * done + 2)

                    @pl.when(reached & trailing)
                    def _():
                        change = three((own_high[rows, inner], own_low[rows, inner]), (high_ref[other, inner], low_ref[other, inner]))
                        state[rows, here] = state[rows, here] - change
        leave[k].start()
    for copy in leave:
        copy.wait()


def finish_own(col_count, fetch, place, slab, own, factor_rows, inverses):
    row_count = slab.shape[0]
    vmem = pl.BlockSpec(memory_space=pltpu.VMEM)
    head_width = -(-HEAD_BLOCKS // col_count) * BLOCK
    half = [jax.ShapeDtypeStruct((row_count, HEAD), jnp.bfloat16)] * 2
    rows = [jax.ShapeDtypeStruct((BLOCK, b * BLOCK), jnp.bfloat16) for b in range(1, HEAD_BLOCKS) for _ in range(2)]
    squares = [jax.ShapeDtypeStruct((BLOCK, BLOCK), jnp.bfloat16)] * (2 * HEAD_BLOCKS)
    return pl.pallas_call(
        functools.partial(own_kernel, col_count, fetch, len(own)),
        out_shape=[jax.ShapeDtypeStruct((row_count, head_width), jnp.float32)] + half + rows + squares,
        in_specs=[pl.BlockSpec(memory_space=pltpu.SMEM)] + [vmem] * (1 + len(own) + 2 * HEAD_BLOCKS),
        compiler_params=pltpu.CompilerParams(vmem_limit_bytes=32 * 2**20),
        cost_estimate=pl.CostEstimate(flops=8_000_000_000, bytes_accessed=2**20, transcendentals=0),
        name="finish_own",
    )(place, slab[:, :head_width], *own, *factor_rows, *inverses)


def finish_mirror(first_slot, col_count, fetch, slot_of, place, slab, mirrored, solved):
    vmem = pl.BlockSpec(memory_space=pltpu.VMEM)
    anywhere = pl.BlockSpec(memory_space=pl.ANY)
    row_count, width = slab.shape
    rows = width - first_slot * BLOCK
    return pl.pallas_call(
        functools.partial(mirror_kernel, first_slot, col_count, fetch, slot_of, len(mirrored)),
        out_shape=jax.ShapeDtypeStruct(slab.shape, jnp.float32),
        in_specs=[pl.BlockSpec(memory_space=pltpu.SMEM), anywhere] + [vmem] * (len(mirrored) + len(solved)),
        out_specs=anywhere,
        scratch_shapes=[
            pltpu.VMEM(slab.shape, jnp.float32),
            pltpu.VMEM((rows, HEAD), jnp.bfloat16),
            pltpu.VMEM((rows, HEAD), jnp.bfloat16),
            pltpu.VMEM((rows, BLOCK), jnp.float32),
            pltpu.SemaphoreType.DMA((width // BLOCK,)),
            pltpu.SemaphoreType.DMA((width // BLOCK,)),
            pltpu.VMEM((BLOCK, BLOCK), jnp.float32),
        ],
        compiler_params=pltpu.CompilerParams(vmem_limit_bytes=40 * 2**20),
        cost_estimate=pl.CostEstimate(flops=10_000_000_000, bytes_accessed=2**23, transcendentals=0),
        name="finish_mirror",
    )(place, slab, *mirrored, *solved)


def after(value, *tokens):
    nothing = jnp.minimum(sum(jnp.abs(token.reshape(-1, BLOCK, BLOCK)[0]) for token in tokens), 0.0)
    return (value.reshape(-1, BLOCK, BLOCK) + nothing).reshape(value.shape)


def gathered(slab):
    row_count, width = slab.shape
    col_count = lax.axis_size("col")
    owners = min(col_count, HEAD_BLOCKS)
    slots = HEAD_BLOCKS // owners
    first_slot = HEAD_BLOCKS // col_count
    own = lax.all_gather(slab[:, : slots * BLOCK], "col")[:owners]
    own = own.reshape(owners, row_count, slots, BLOCK).transpose(2, 0, 1, 3).reshape(HEAD_BLOCKS, row_count, BLOCK)
    devices = HEAD // row_count
    head = lax.all_gather(own, "row")[:devices].transpose(0, 2, 1, 3).reshape(HEAD_BLOCKS, BLOCK, HEAD)
    mirror = lax.all_gather(slab[:, first_slot * BLOCK :], "row")[:devices]
    mirror = mirror.reshape(HEAD, width - first_slot * BLOCK).T.reshape(-1, BLOCK, HEAD)

    def head_block(row, col, refs, index, b):
        return refs[0][:, b * BLOCK : (b + 1) * BLOCK]

    def mirror_block(row, col, refs, i, b):
        return refs[0][i, :, b * BLOCK : (b + 1) * BLOCK]

    def own_block(row, col, refs, b):
        return refs[0][b]

    def raw(b, inverses):
        return [head[b]], []

    def complete(token):
        return [own], [mirror]

    return raw, [head_block] * HEAD_BLOCKS, complete, own_block, mirror_block, lambda row, i: i


def exchanged(slab):
    row_count, width = slab.shape
    col_count = lax.axis_size("col")
    cores = 2
    ys = col_count // cores
    xs = ys
    zs = lax.axis_size("row") // xs
    r, c = lax.axis_index("row"), lax.axis_index("col")
    z, x, y, core = r // xs, r % xs, c // cores, c % cores
    tile = slab[:, :BLOCK]
    top, bottom = tile[:BLOCK], tile[BLOCK:]
    spots = [(a, b, e) for a in range(xs) for b in range(ys) for e in range(cores)]
    everyone = [(k, *spot) for k in range(zs) for spot in spots]

    def flat(z, x, y, core):
        return (z * xs + x) * col_count + y * cores + core

    def send(value, pairs):
        return lax.ppermute(value, ("row", "col"), [(flat(*a), flat(*b)) for a, b in pairs])

    def swap_core(value):
        return send(value, [((k, a, b, e), (k, a, b, 1 - e)) for k, a, b, e in everyone])

    def swap_x(value):
        return send(value, [((k, a, b, e), (k, 1 - a, b, e)) for k, a, b, e in everyone])

    def swap_y(value):
        return send(value, [((k, a, b, e), (k, a, 1 - b, e)) for k, a, b, e in everyone])

    def down(value, sources, steps=None):
        stride = zs // 2
        have = [0]
        while stride:
            came = send(value, [((k, *s), (k + stride, *s)) for k in have for s in sources])
            value = jnp.where(functools.reduce(jnp.logical_or, [z == k for k in have]), value, came)
            have = have + [k + stride for k in have]
            stride //= 2
            if steps is not None:
                steps.append(value)
        return value

    def spread(value, sources):
        came = send(value, [((k, 0, 0, e), (k, 1, 0, e)) for k in range(zs) for e in sources])
        value = jnp.where(x == 0, value, came)
        came = send(value, [((k, a, 0, e), (k, a, 1, e)) for k in range(zs) for a in range(xs) for e in sources])
        return jnp.where(y == 0, value, came)

    zero_z = down(top, [(0, 0, 0)])
    zero_here = spread(zero_z, [0])
    zero = send(zero_here, [((k, a, b, 0), (k, a, b, 1)) for k, a, b, e in everyone if e == 0])
    zero = jnp.where(core == 0, zero_here, zero)
    one_here = spread(down(bottom, [(0, 0, 0), (0, 0, 1)]), [0, 1])
    rest_steps = []
    came = send(top, [((0, 1, b, e), (0, 0, b, e)) for b in range(ys) for e in range(cores)])
    rest_here = down(jnp.where(x == 0, after(came, zero_z), bottom), spots, rest_steps)
    steps = zs - 1
    turned = send(tile, [((k, a, 1 - a, e), (k, 1 - a, a, e)) for k in range(1, zs) for a in range(xs) for e in range(cores)])
    part = jnp.where(x == y, tile, after(turned, zero_here))
    passed = [part]
    for shift in range(1, steps):
        passed.append(
            send(part, [((1 + k, *s), (1 + (k + shift) % steps, *s)) for k in range(steps) for s in spots])
        )
    mirrored = []

    def mirror(shift, token):
        held = jnp.where(z == 0, slab[:, (1 + shift) * BLOCK : (2 + shift) * BLOCK], after(passed[shift], token))
        mirrored.append([held, swap_x(held)])

    kept = {}

    def raw(b, inverses):
        if b == 0:
            return [zero], [turned, rest_here]
        if b == 1:
            one = after(one_here, inverses[0])
            one_other = swap_core(one)
            flips = []
            mirror(0, zero_here)
            later = after(rest_here, one_other, passed[1], mirrored[0][1])
            for dx, dy in ((1, 1), (1, 0), (0, 1)):
                flips.append(send(later, [((k, i, j, e), (k, i ^ dx, j ^ dy, e)) for k, i, j, e in everyone]))
            kept["rest"] = [later, flips[1], flips[2], flips[0]]
            return [one, one_other], []
        if b == 2:
            rest = after(jnp.stack(kept["rest"], 0), inverses[1], *passed[2:])
            rest_other = swap_core(rest)
            kept["rest"] = [rest, rest_other]
            for shift in range(1, steps):
                mirror(shift, rest_other[0])
            kept["own"] = swap_y(after(tile, rest_other[0]))
            return kept["rest"], []
        return kept["rest"], []

    def complete(token):
        own = [tile, kept["own"], swap_core(tile), swap_core(kept["own"])]
        pieces = [value for pair in mirrored for value in pair]
        give = jnp.stack([jnp.where(core == 0, value[BLOCK:], value[:BLOCK]) for value in pieces], 0)
        return own, pieces + [swap_core(after(give, token))]

    def here(row, col):
        return row // xs, row % xs, col // cores, col % cores

    def first_block(row, col, refs, index, b):
        return refs[0][...]

    def second_block(row, col, refs, index, b):
        return jnp.where(here(row, col)[3] == b, refs[0][...], refs[1][...])

    def rest_block(row, col, refs, index, b):
        z, x, y, core = here(row, col)
        place = jnp.where(y == b // cores, 0, 2) + jnp.where(x == index - 2, 0, 1)
        return jnp.where(core == b % cores, refs[0][place], refs[1][place])

    def mirror_block(row, col, refs, i, b):
        z, x, y, core = here(row, col)
        got, stage = refs[2 * steps :]
        same_x = x == b // cores

        @pl.when(z == 0)
        def _():
            rows = slice((b % cores) * BLOCK, (b % cores + 1) * BLOCK)
            stage[...] = jnp.where(same_x, refs[2 * i][rows, :], refs[2 * i + 1][rows, :]).T

        @pl.when(z != 0)
        def _():
            rows = pl.ds(pl.multiple_of(core * BLOCK, BLOCK), BLOCK)
            near = jnp.where(same_x, refs[2 * i][rows, :], refs[2 * i + 1][rows, :])
            stage[...] = jnp.where(core == b % cores, near, got[2 * i + jnp.where(same_x, 0, 1)])

        return stage[...]

    def own_block(row, col, refs, b):
        z, x, y, core = here(row, col)
        same = jnp.where(y == b // cores, refs[0][...], refs[1][...])
        other = jnp.where(y == b // cores, refs[2][...], refs[3][...])
        return jnp.where(core == b % cores, same, other)

    def slot_of(row, i):
        z = row // xs
        return jnp.where(z == 0, i, lax.rem(z - 1 - i + steps, steps))

    fetch_mirror, fetch_own = mirror_block, own_block
    return raw, [first_block, second_block, rest_block, rest_block], complete, fetch_own, fetch_mirror, slot_of


def shards(slab):
    row_count, width = slab.shape
    row_total, col_count = lax.axis_size("row"), lax.axis_size("col")
    slots = width // BLOCK
    fits = (
        row_count == 2 * BLOCK
        and col_count == HEAD_BLOCKS
        and slots > 1
        and slots & (slots - 1) == 0
        and row_total == (col_count // 2) * slots
    )
    raw, fetch, complete, own_fetch, mirror_fetch, slot_of = exchanged(slab) if fits else gathered(slab)
    place = jnp.stack([lax.axis_index("row"), lax.axis_index("col")]).astype(jnp.int32)
    factor_rows, inverses = [], []
    for b in range(HEAD_BLOCKS):
        pieces, ready = raw(b, inverses)
        row, inverse = head_row(b, fetch[b], place, pieces, ready, factor_rows, inverses)
        factor_rows.append(row)
        inverses.append(inverse)
    own, mirrored = complete(inverses[-1])
    solved = finish_own(col_count, own_fetch, place, slab, own, factor_rows, inverses)
    return finish_mirror(HEAD_BLOCKS // col_count, col_count, mirror_fetch, slot_of, place, slab, mirrored, solved)


def solution(mesh):
    in_specs = (P("row", "col"),)
    out_specs = P("row", "col")
    return jax.shard_map(shards, mesh=mesh, in_specs=in_specs, out_specs=out_specs, check_vma=False)
```

```python
import functools

import jax
import jax.numpy as jnp
from jax import lax
from jax.experimental import pallas as pl
from jax.experimental.pallas import tpu as pltpu
from jax.sharding import PartitionSpec as P

BLOCK = 256
PANELS = 2
LEAF = 128
SUB = 8
HEAD_BLOCKS = 2 * PANELS
HEAD = HEAD_BLOCKS * BLOCK
HEAD_COST = 10_000_000_000
NT = (((1,), (1,)), ((), ()))
NN = (((1,), (0,)), ((), ()))


def exact(left_side, right_side, dims=NT):
    return lax.dot_general(left_side, right_side, dims, precision=lax.Precision.HIGHEST, preferred_element_type=jnp.float32)


def split(value):
    high = value.astype(jnp.bfloat16)
    low = (value - high.astype(jnp.float32)).astype(jnp.bfloat16)
    return high, low


def three(left_side, right_side):
    def dot(a, b):
        return lax.dot_general(a, b, NT, preferred_element_type=jnp.float32)
    return dot(left_side[0], right_side[1]) + dot(left_side[1], right_side[0]) + dot(left_side[0], right_side[0])


def lane(value, index):
    return jnp.broadcast_to(value[:, index : index + 1], (SUB, LEAF))


def sublane(value, index):
    return jnp.broadcast_to(value[index : index + 1, :], (SUB, LEAF))


def leaf(block):
    groups = LEAF // SUB
    rows = lax.broadcasted_iota(jnp.int32, (SUB, LEAF), 0)
    cols = lax.broadcasted_iota(jnp.int32, (SUB, LEAF), 1)
    left = [block[SUB * g : SUB * g + SUB, :] for g in range(groups)]
    right = [jnp.where(cols == rows + SUB * g, 1.0, 0.0).astype(jnp.float32) for g in range(groups)]
    upper, inverse = [], []
    for p in range(groups):
        columns = [lane(left[p], SUB * p + j) for j in range(SUB)]
        here_left, here_right = left[p], right[p]
        pivots, rows_left, rows_right, heads = [], [], [], []
        scale = jnp.zeros((SUB, LEAF), jnp.float32)
        for j in range(SUB):
            root = lax.rsqrt(sublane(columns[j], j))
            pivot = root * root
            scale = jnp.where(rows == j, root, scale)
            below = jnp.where(rows > j, columns[j], 0.0)
            factor = below * pivot
            row_left, row_right = sublane(here_left, j), sublane(here_right, j)
            head = {l: sublane(columns[l], j) for l in range(j + 1, SUB)}
            if j + 1 < SUB:
                columns[j + 1] = columns[j + 1] - (below * root) * (head[j + 1] * root)
            for l in range(j + 2, SUB):
                columns[l] = columns[l] - factor * head[l]
            here_left = here_left - factor * row_left
            here_right = here_right - factor * row_right
            pivots.append(pivot)
            rows_left.append(row_left)
            rows_right.append(row_right)
            heads.append(head)
        upper.append(jnp.where(cols >= rows + SUB * p, here_left * scale, 0.0))
        inverse.append(here_right * scale)
        for g in range(p + 1, groups):
            columns = [lane(left[g], SUB * p + j) for j in range(SUB)]
            for j in range(SUB):
                factor = columns[j] * pivots[j]
                for l in range(j + 1, SUB):
                    columns[l] = columns[l] - factor * heads[j][l]
                left[g] = left[g] - factor * rows_left[j]
                right[g] = right[g] - factor * rows_right[j]
    return jnp.concatenate(upper, 0), jnp.concatenate(inverse, 0)


def head_row_kernel(index, fetch, pieces, ready, place_ref, *refs):
    raw = refs[:pieces]
    above = refs[pieces : pieces + index]
    inverses = refs[pieces + index : pieces + 2 * index]
    row_ref, inverse_ref, work = refs[pieces + 2 * index + ready :]
    here = slice(index * BLOCK, (index + 1) * BLOCK)
    block_of = functools.partial(fetch, place_ref[0], place_ref[1], raw, index)
    for b in range(index):
        block = block_of(b)
        if b:
            block = block - exact(row_ref[:, : b * BLOCK], above[b][:, : b * BLOCK])
        row_ref[:, b * BLOCK : (b + 1) * BLOCK] = exact(block, inverses[b][...])
    diagonal = block_of(index)
    if index:
        solved = row_ref[:, : index * BLOCK]
        diagonal = diagonal - exact(solved, solved)
    work[...] = diagonal
    row_ref[:, here] = jnp.zeros((BLOCK, BLOCK), jnp.float32)
    inverse_ref[...] = jnp.zeros((BLOCK, BLOCK), jnp.float32)
    start = index * BLOCK

    def step(i, carry):
        place = pl.ds(pl.multiple_of(i * LEAF, LEAF), LEAF)
        upper, inverse = leaf(work[place, place])
        row_ref[place, pl.ds(pl.multiple_of(start + i * LEAF, LEAF), LEAF)] = upper.T
        inverse_ref[place, place] = inverse

        @pl.when(i == 0)
        def _():
            below = exact(work[LEAF:, :LEAF], inverse)
            row_ref[LEAF:, start : start + LEAF] = below
            work[LEAF:, LEAF:] = work[LEAF:, LEAF:] - exact(below, below)
            work[LEAF:, :LEAF] = exact(below, inverse, NN)

        @pl.when(i == 1)
        def _():
            inverse_ref[LEAF:, :LEAF] = -exact(inverse, work[LEAF:, :LEAF], NN)

        return carry

    lax.fori_loop(0, BLOCK // LEAF, step, 0)


def head_row(index, fetch, place, raw, ready, above, inverses):
    return pl.pallas_call(
        functools.partial(head_row_kernel, index, fetch, len(raw), len(ready)),
        out_shape=[
            jax.ShapeDtypeStruct((BLOCK, (index + 1) * BLOCK), jnp.float32),
            jax.ShapeDtypeStruct((BLOCK, BLOCK), jnp.float32),
        ],
        in_specs=[pl.BlockSpec(memory_space=pltpu.SMEM)] + [pl.BlockSpec(memory_space=pltpu.VMEM)] * (len(raw) + 2 * index)
        + [pl.BlockSpec(memory_space=pl.ANY)] * len(ready),
        scratch_shapes=[pltpu.VMEM((BLOCK, BLOCK), jnp.float32)],
        compiler_params=pltpu.CompilerParams(vmem_limit_bytes=24 * 2**20),
        cost_estimate=pl.CostEstimate(flops=HEAD_COST, bytes_accessed=2**20, transcendentals=0),
        name=f"head_row_{index}",
    )(place, *raw, *above, *inverses, *ready)


def solve(fetch, high_ref, low_ref, row_splits, inverse_splits, store=None):
    for b in range(HEAD_BLOCKS):
        here, done = slice(b * BLOCK, (b + 1) * BLOCK), slice(0, b * BLOCK)
        value = fetch(b)
        if b:
            value = value - three((high_ref[:, done], low_ref[:, done]), row_splits[b])
        solved = three(split(value), inverse_splits[b])
        if store is not None:
            store(b, solved)
        high, low = split(solved)
        high_ref[:, here] = high
        low_ref[:, here] = low


def own_kernel(col_count, fetch, owned, place_ref, slab_ref, *refs):
    own = refs[:owned]
    factor_rows = refs[owned : owned + HEAD_BLOCKS]
    inverses = refs[owned + HEAD_BLOCKS : owned + 2 * HEAD_BLOCKS]
    outs = refs[owned + 2 * HEAD_BLOCKS :]
    column_ref, high_ref, low_ref = outs[:3]
    row_refs, inverse_refs = outs[3 : 1 + 2 * HEAD_BLOCKS], outs[1 + 2 * HEAD_BLOCKS :]
    row_count = high_ref.shape[0]
    row_index, col_index = place_ref[0], place_ref[1]
    first_row_block = row_index * (row_count // BLOCK)
    column_ref[...] = slab_ref[:, : column_ref.shape[1]]
    row_splits, inverse_splits = [None], []
    for b in range(HEAD_BLOCKS):
        if b:
            row_splits.append(split(factor_rows[b][:, : b * BLOCK]))
            row_refs[2 * b - 2][...], row_refs[2 * b - 1][...] = row_splits[b]
        inverse_splits.append(split(inverses[b][...]))
        inverse_refs[2 * b][...], inverse_refs[2 * b + 1][...] = inverse_splits[b]

    def store(b, solved):
        slot = slice(b // col_count * BLOCK, (b // col_count + 1) * BLOCK)

        @pl.when(col_index == b % col_count)
        def _():
            diagonal = factor_rows[b][:, b * BLOCK : (b + 1) * BLOCK]
            for i in range(row_count // BLOCK):
                rows = slice(i * BLOCK, (i + 1) * BLOCK)
                block = first_row_block + i
                column_ref[rows, slot] = jnp.where(block == b, diagonal, jnp.where(block < b, 0.0, solved[rows]))

    solve(lambda b: fetch(row_index, col_index, own, b), high_ref, low_ref, row_splits, inverse_splits, store)


def mirror_kernel(first_slot, col_count, fetch, slot_of, pieces, place_ref, slab_ref, *refs):
    mirrored = refs[:pieces] + refs[-1:]
    column_ref, own_high, own_low = refs[pieces : pieces + 3]
    splits = refs[pieces + 3 : pieces + 1 + 4 * HEAD_BLOCKS]
    row_refs, inverse_refs = splits[: 2 * HEAD_BLOCKS - 2], splits[2 * HEAD_BLOCKS - 2 :]
    out_ref, state, high_ref, low_ref, raw_ref, into, outof, _ = refs[pieces + 1 + 4 * HEAD_BLOCKS :]
    row_count, width = slab_ref.shape
    row_index, col_index = place_ref[0], place_ref[1]
    first_row_block = row_index * (row_count // BLOCK)
    slots = range(width // BLOCK)
    arrive = [
        pltpu.make_async_copy(slab_ref.at[:, k * BLOCK : (k + 1) * BLOCK], state.at[:, k * BLOCK : (k + 1) * BLOCK], into.at[k])
        for k in slots
    ]
    leave = [
        pltpu.make_async_copy(state.at[:, k * BLOCK : (k + 1) * BLOCK], out_ref.at[:, k * BLOCK : (k + 1) * BLOCK], outof.at[k])
        for k in slots
    ]
    for copy in arrive:
        copy.start()
    count = width // BLOCK - first_slot
    places = [pl.ds(pl.multiple_of(slot_of(row_index, i) * BLOCK, BLOCK), BLOCK) for i in range(count)]

    def block_of(b):
        for i in range(count):
            raw_ref[places[i], :] = fetch(row_index, col_index, mirrored, i, b)
        return raw_ref[...]

    row_splits = [None] + [(row_refs[2 * b - 2][...], row_refs[2 * b - 1][...]) for b in range(1, HEAD_BLOCKS)]
    inverse_splits = [(inverse_refs[2 * b][...], inverse_refs[2 * b + 1][...]) for b in range(HEAD_BLOCKS)]
    solve(block_of, high_ref, low_ref, row_splits, inverse_splits)
    panel = 2 * BLOCK
    head_slots = column_ref.shape[1] // BLOCK
    for k in slots:
        arrive[k].wait()
        here = slice(k * BLOCK, (k + 1) * BLOCK)
        if k < head_slots:
            state[:, here] = column_ref[:, here]
        if k >= first_slot:
            other = slice((k - first_slot) * BLOCK, (k - first_slot + 1) * BLOCK)
            trailing = k * col_count + col_index >= HEAD_BLOCKS
            last = first_row_block >= HEAD_BLOCKS

            @pl.when(last & trailing)
            def _():
                change = three((own_high[...], own_low[...]), (high_ref[other, :], low_ref[other, :]))
                state[:, here] = state[:, here] - change

            for i in range(row_count // BLOCK):
                rows = slice(i * BLOCK, (i + 1) * BLOCK)
                for done in range(1, PANELS + 1):
                    inner = slice(0, done * panel)
                    block = first_row_block + i
                    reached = (block >= 2 * done) & (first_row_block < HEAD_BLOCKS)
                    if done < PANELS:
                        reached = reached & (block < 2 * done + 2)

                    @pl.when(reached & trailing)
                    def _():
                        change = three((own_high[rows, inner], own_low[rows, inner]), (high_ref[other, inner], low_ref[other, inner]))
                        state[rows, here] = state[rows, here] - change
        leave[k].start()
    for copy in leave:
        copy.wait()


def finish_own(col_count, fetch, place, slab, own, factor_rows, inverses):
    row_count = slab.shape[0]
    vmem = pl.BlockSpec(memory_space=pltpu.VMEM)
    head_width = -(-HEAD_BLOCKS // col_count) * BLOCK
    half = [jax.ShapeDtypeStruct((row_count, HEAD), jnp.bfloat16)] * 2
    rows = [jax.ShapeDtypeStruct((BLOCK, b * BLOCK), jnp.bfloat16) for b in range(1, HEAD_BLOCKS) for _ in range(2)]
    squares = [jax.ShapeDtypeStruct((BLOCK, BLOCK), jnp.bfloat16)] * (2 * HEAD_BLOCKS)
    return pl.pallas_call(
        functools.partial(own_kernel, col_count, fetch, len(own)),
        out_shape=[jax.ShapeDtypeStruct((row_count, head_width), jnp.float32)] + half + rows + squares,
        in_specs=[pl.BlockSpec(memory_space=pltpu.SMEM)] + [vmem] * (1 + len(own) + 2 * HEAD_BLOCKS),
        compiler_params=pltpu.CompilerParams(vmem_limit_bytes=32 * 2**20),
        cost_estimate=pl.CostEstimate(flops=8_000_000_000, bytes_accessed=2**20, transcendentals=0),
        name="finish_own",
    )(place, slab[:, :head_width], *own, *factor_rows, *inverses)


def finish_mirror(first_slot, col_count, fetch, slot_of, place, slab, mirrored, solved):
    vmem = pl.BlockSpec(memory_space=pltpu.VMEM)
    anywhere = pl.BlockSpec(memory_space=pl.ANY)
    row_count, width = slab.shape
    rows = width - first_slot * BLOCK
    return pl.pallas_call(
        functools.partial(mirror_kernel, first_slot, col_count, fetch, slot_of, len(mirrored)),
        out_shape=jax.ShapeDtypeStruct(slab.shape, jnp.float32),
        in_specs=[pl.BlockSpec(memory_space=pltpu.SMEM), anywhere] + [vmem] * (len(mirrored) + len(solved)),
        out_specs=anywhere,
        scratch_shapes=[
            pltpu.VMEM(slab.shape, jnp.float32),
            pltpu.VMEM((rows, HEAD), jnp.bfloat16),
            pltpu.VMEM((rows, HEAD), jnp.bfloat16),
            pltpu.VMEM((rows, BLOCK), jnp.float32),
            pltpu.SemaphoreType.DMA((width // BLOCK,)),
            pltpu.SemaphoreType.DMA((width // BLOCK,)),
            pltpu.VMEM((BLOCK, BLOCK), jnp.float32),
        ],
        compiler_params=pltpu.CompilerParams(vmem_limit_bytes=40 * 2**20),
        cost_estimate=pl.CostEstimate(flops=10_000_000_000, bytes_accessed=2**23, transcendentals=0),
        name="finish_mirror",
    )(place, slab, *mirrored, *solved)


def after(value, *tokens):
    nothing = jnp.minimum(sum(jnp.abs(token.reshape(-1, BLOCK, BLOCK)[0]) for token in tokens), 0.0)
    return (value.reshape(-1, BLOCK, BLOCK) + nothing).reshape(value.shape)


def gathered(slab):
    row_count, width = slab.shape
    col_count = lax.axis_size("col")
    owners = min(col_count, HEAD_BLOCKS)
    slots = HEAD_BLOCKS // owners
    first_slot = HEAD_BLOCKS // col_count
    own = lax.all_gather(slab[:, : slots * BLOCK], "col")[:owners]
    own = own.reshape(owners, row_count, slots, BLOCK).transpose(2, 0, 1, 3).reshape(HEAD_BLOCKS, row_count, BLOCK)
    devices = HEAD // row_count
    head = lax.all_gather(own, "row")[:devices].transpose(0, 2, 1, 3).reshape(HEAD_BLOCKS, BLOCK, HEAD)
    mirror = lax.all_gather(slab[:, first_slot * BLOCK :], "row")[:devices]
    mirror = mirror.reshape(HEAD, width - first_slot * BLOCK).T.reshape(-1, BLOCK, HEAD)

    def head_block(row, col, refs, index, b):
        return refs[0][:, b * BLOCK : (b + 1) * BLOCK]

    def mirror_block(row, col, refs, i, b):
        return refs[0][i, :, b * BLOCK : (b + 1) * BLOCK]

    def own_block(row, col, refs, b):
        return refs[0][b]

    def raw(b, inverses):
        return [head[b]], []

    def complete(token):
        return [own], [mirror]

    return raw, [head_block] * HEAD_BLOCKS, complete, own_block, mirror_block, lambda row, i: i


def exchanged(slab):
    row_count, width = slab.shape
    col_count = lax.axis_size("col")
    cores = 2
    ys = col_count // cores
    xs = ys
    zs = lax.axis_size("row") // xs
    r, c = lax.axis_index("row"), lax.axis_index("col")
    z, x, y, core = r // xs, r % xs, c // cores, c % cores
    tile = slab[:, :BLOCK]
    top, bottom = tile[:BLOCK], tile[BLOCK:]
    spots = [(a, b, e) for a in range(xs) for b in range(ys) for e in range(cores)]
    everyone = [(k, *spot) for k in range(zs) for spot in spots]

    def flat(z, x, y, core):
        return (z * xs + x) * col_count + y * cores + core

    def send(value, pairs):
        return lax.ppermute(value, ("row", "col"), [(flat(*a), flat(*b)) for a, b in pairs])

    def swap_core(value):
        return send(value, [((k, a, b, e), (k, a, b, 1 - e)) for k, a, b, e in everyone])

    def swap_x(value):
        return send(value, [((k, a, b, e), (k, 1 - a, b, e)) for k, a, b, e in everyone])

    def swap_y(value):
        return send(value, [((k, a, b, e), (k, a, 1 - b, e)) for k, a, b, e in everyone])

    def down(value, sources, steps=None):
        stride = zs // 2
        have = [0]
        while stride:
            came = send(value, [((k, *s), (k + stride, *s)) for k in have for s in sources])
            value = jnp.where(functools.reduce(jnp.logical_or, [z == k for k in have]), value, came)
            have = have + [k + stride for k in have]
            stride //= 2
            if steps is not None:
                steps.append(value)
        return value

    def spread(value, sources):
        came = send(value, [((k, 0, 0, e), (k, 1, 0, e)) for k in range(zs) for e in sources])
        value = jnp.where(x == 0, value, came)
        came = send(value, [((k, a, 0, e), (k, a, 1, e)) for k in range(zs) for a in range(xs) for e in sources])
        return jnp.where(y == 0, value, came)

    zero_z = down(top, [(0, 0, 0)])
    zero_here = spread(zero_z, [0])
    zero = send(zero_here, [((k, a, b, 0), (k, a, b, 1)) for k, a, b, e in everyone if e == 0])
    zero = jnp.where(core == 0, zero_here, zero)
    one_here = spread(down(bottom, [(0, 0, 0), (0, 0, 1)]), [0, 1])
    rest_steps = []
    came = send(top, [((0, 1, b, e), (0, 0, b, e)) for b in range(ys) for e in range(cores)])
    rest_here = down(jnp.where(x == 0, after(came, zero_z), bottom), spots, rest_steps)
    steps = zs - 1
    turned = send(tile, [((k, a, 1 - a, e), (k, 1 - a, a, e)) for k in range(1, zs) for a in range(xs) for e in range(cores)])
    part = jnp.where(x == y, tile, after(turned, zero_here))
    passed = [part]
    for shift in range(1, steps):
        passed.append(
            send(part, [((1 + k, *s), (1 + (k + shift) % steps, *s)) for k in range(steps) for s in spots])
        )
    mirrored = []

    def mirror(shift, token):
        held = jnp.where(z == 0, slab[:, (1 + shift) * BLOCK : (2 + shift) * BLOCK], after(passed[shift], token))
        mirrored.append([held, swap_x(held)])

    kept = {}

    def raw(b, inverses):
        if b == 0:
            return [zero], [turned, rest_here]
        if b == 1:
            one = after(one_here, inverses[0])
            one_other = swap_core(one)
            flips = []
            mirror(0, zero_here)
            later = after(rest_here, one_other, passed[1], mirrored[0][1])
            for dx, dy in ((1, 1), (1, 0), (0, 1)):
                flips.append(send(later, [((k, i, j, e), (k, i ^ dx, j ^ dy, e)) for k, i, j, e in everyone]))
            kept["rest"] = [later, flips[1], flips[2], flips[0]]
            return [one, one_other], []
        if b == 2:
            rest = after(jnp.stack(kept["rest"], 0), inverses[1], *passed[2:])
            rest_other = swap_core(rest)
            kept["rest"] = [rest, rest_other]
            for shift in range(1, steps):
                mirror(shift, rest_other[0])
            kept["own"] = swap_y(after(tile, rest_other[0]))
            kept["tile"] = swap_core(after(tile, inverses[0]))
            return kept["rest"], [kept["tile"]]
        return kept["rest"], [kept["tile"]]

    def complete(token):
        own = [tile, kept["own"], kept["tile"], swap_core(kept["own"])]
        pieces = [value for pair in mirrored for value in pair]
        give = jnp.stack([jnp.where(core == 0, value[BLOCK:], value[:BLOCK]) for value in pieces], 0)
        return own, pieces + [swap_core(after(give, token))]

    def here(row, col):
        return row // xs, row % xs, col // cores, col % cores

    def first_block(row, col, refs, index, b):
        return refs[0][...]

    def second_block(row, col, refs, index, b):
        return jnp.where(here(row, col)[3] == b, refs[0][...], refs[1][...])

    def rest_block(row, col, refs, index, b):
        z, x, y, core = here(row, col)
        place = jnp.where(y == b // cores, 0, 2) + jnp.where(x == index - 2, 0, 1)
        return jnp.where(core == b % cores, refs[0][place], refs[1][place])

    def mirror_block(row, col, refs, i, b):
        z, x, y, core = here(row, col)
        got, stage = refs[2 * steps :]
        same_x = x == b // cores

        @pl.when(z == 0)
        def _():
            rows = slice((b % cores) * BLOCK, (b % cores + 1) * BLOCK)
            stage[...] = jnp.where(same_x, refs[2 * i][rows, :], refs[2 * i + 1][rows, :]).T

        @pl.when(z != 0)
        def _():
            rows = pl.ds(pl.multiple_of(core * BLOCK, BLOCK), BLOCK)
            near = jnp.where(same_x, refs[2 * i][rows, :], refs[2 * i + 1][rows, :])
            stage[...] = jnp.where(core == b % cores, near, got[2 * i + jnp.where(same_x, 0, 1)])

        return stage[...]

    def own_block(row, col, refs, b):
        z, x, y, core = here(row, col)
        same = jnp.where(y == b // cores, refs[0][...], refs[1][...])
        other = jnp.where(y == b // cores, refs[2][...], refs[3][...])
        return jnp.where(core == b % cores, same, other)

    def slot_of(row, i):
        z = row // xs
        return jnp.where(z == 0, i, lax.rem(z - 1 - i + steps, steps))

    fetch_mirror, fetch_own = mirror_block, own_block
    return raw, [first_block, second_block, rest_block, rest_block], complete, fetch_own, fetch_mirror, slot_of


def shards(slab):
    row_count, width = slab.shape
    row_total, col_count = lax.axis_size("row"), lax.axis_size("col")
    slots = width // BLOCK
    fits = (
        row_count == 2 * BLOCK
        and col_count == HEAD_BLOCKS
        and slots > 1
        and slots & (slots - 1) == 0
        and row_total == (col_count // 2) * slots
    )
    raw, fetch, complete, own_fetch, mirror_fetch, slot_of = exchanged(slab) if fits else gathered(slab)
    place = jnp.stack([lax.axis_index("row"), lax.axis_index("col")]).astype(jnp.int32)
    factor_rows, inverses = [], []
    for b in range(HEAD_BLOCKS):
        pieces, ready = raw(b, inverses)
        row, inverse = head_row(b, fetch[b], place, pieces, ready, factor_rows, inverses)
        factor_rows.append(row)
        inverses.append(inverse)
    own, mirrored = complete(inverses[-1])
    solved = finish_own(col_count, own_fetch, place, slab, own, factor_rows, inverses)
    return finish_mirror(HEAD_BLOCKS // col_count, col_count, mirror_fetch, slot_of, place, slab, mirrored, solved)


def solution(mesh):
    in_specs = (P("row", "col"),)
    out_specs = P("row", "col")
    return jax.shard_map(shards, mesh=mesh, in_specs=in_specs, out_specs=out_specs, check_vma=False)
```
